32 devices in a mesh: node: 4 (over y, core), local: 8 (over z, x).
Axes of the slice: x: 2, y: 2, z: 4, core: 2. Of those that a mesh axis runs over, the one named last changes fastest.
Arguments:
- tokens: bfloat16 [4096, 3584], P(('node', 'local')), may hold values from -3 to 3
- act_scale: float32 [4096, 28], P(('node', 'local')), may hold values from 0.25 to 4, as said below
- routes: int32 [4096, 8], P(('node', 'local')), may hold values from 0 to 31, all different within a row; in each aligned block of 128 rows (0 to 127, 128 to 255, ...) at most 40 rows name the same one
- combine: float32 [4096, 8], P(('node', 'local')), may hold values from 0.1 to 0.6
- w_gate: bfloat16 [32, 3584, 1024], P(('node', 'local')), may hold values from -0.046875 to 0.046875
- gate_scale: float32 [32, 28, 8], P(('node', 'local')), may hold values from 0.25 to 4, as said below
- w_up: bfloat16 [32, 3584, 1024], P(('node', 'local')), may hold values from -0.046875 to 0.046875
- up_scale: float32 [32, 28, 8], P(('node', 'local')), may hold values from 0.25 to 4, as said below
- w_down: bfloat16 [32, 1024, 3584], P(('node', 'local')), may hold values from -0.09375 to 0.09375
- down_scale: float32 [32, 8, 28], P(('node', 'local')), may hold values from 0.25 to 4, as said below
Outputs:
- combined: bfloat16 [4096, 3584], P(('node', 'local'))
The draws below stay inside these ranges and needn't reach their ends.
Inputs may be any that keep to these rules, and one draw needn't show every extreme that they name: `routes`: each token names 8 different experts. Among the 128 tokens of one device (aligned blocks), no expert is named more than 40 times, and in some blocks one expert is named exactly 40 times. `act_scale`: every entry is a power of two. `gate_scale`: every entry is a power of two. `up_scale`: every entry is a power of two. `down_scale`: every entry is a power of two.
All inputs are finite; a program needn't handle non-finite values.
Results may differ from the reference program's by a relative error of at most 0.0058.
Values may be sent and summed in bfloat16 or wider, within the bound.
A program may use at most 192 MiB of HBM per device.

```python
import math
import jax
import jax.numpy as jnp
import numpy as np
from jax import lax

D = 3584
FF = 1024
TOP = 8
BLOCK = 128
TOK_DEV = 128
EXPERTS = 32
CAP = 40
TOKENS = 4096


def power_table(key, shape):
    exponent = jax.random.randint(key, shape, -2, 3)
    return jnp.exp2(exponent.astype(jnp.float32))


def draw_act_scale(key, part):
    return power_table(jax.random.fold_in(key, 11), (TOKENS, D // BLOCK))


def draw_gate_scale(key, part):
    return power_table(jax.random.fold_in(key, 23), (EXPERTS, D // BLOCK, FF // BLOCK))


def draw_up_scale(key, part):
    return power_table(jax.random.fold_in(key, 37), (EXPERTS, D // BLOCK, FF // BLOCK))


def draw_down_scale(key, part):
    return power_table(jax.random.fold_in(key, 41), (EXPERTS, FF // BLOCK, D // BLOCK))


def shard_levels(own_key, extent, pieces, low, top_value):
    level, own = 1.0, jax.random.fold_in(own_key, 6)
    for axis_at, blocks in pieces:
        steps = jnp.exp(jax.random.uniform(jax.random.fold_in(own, axis_at), (blocks,), jnp.float32, low / len(pieces), top_value / len(pieces)))
        level = level * jnp.repeat(steps, extent[axis_at] // blocks).reshape([-1 if axis == axis_at else 1 for axis in range(len(extent))])
    return level


def assign_block(stream_key, own, number, rows, amount, top, reach, lean):
    order = jax.random.permutation(stream_key, amount)
    packed, common = load_shares(amount, rows * top, reach, lean, True), load_shares(amount, rows * top, reach, lean, False)
    places = jnp.arange(amount)

    def named(tallies, offset_by):
        used = int((tallies > 0).sum())
        fixed = max(1, used // 4)
        passed = fixed + (places - fixed + offset_by * (used - fixed)) % max(1, amount - fixed)
        return jnp.zeros((amount,), jnp.int32).at[order[jnp.where(places < fixed, places, passed)]].set(jnp.asarray(tallies, jnp.int32))

    tallies = jnp.where(number % 4 == 0, named(packed, number // 4), named(common, number - number // 4 - 1))
    mixed = jax.random.permutation(jax.random.fold_in(own, 3), amount)
    donor, receiver = mixed[0:amount // 2 * 2:2], mixed[1:amount // 2 * 2:2]
    slack = jnp.minimum(tallies[donor] - 1, reach - tallies[receiver]) // 2
    slack = jnp.where((donor == order[0]) | (receiver == order[0]) | (tallies[receiver] == 0), 0, jnp.maximum(slack, 0))
    passed = jax.random.randint(jax.random.fold_in(own, 4), (amount // 2,), 0, 1 << 20) % (slack + 1)
    tallies = tallies.at[donor].add(-passed).at[receiver].add(passed)
    labels = jnp.searchsorted(jnp.cumsum(tallies), jnp.arange(rows * top), side="right").astype(jnp.int32)
    grid = labels.reshape(top, rows).T
    grid = grid[jax.random.permutation(jax.random.fold_in(own, 1), rows)]
    offset_by = jax.random.randint(jax.random.fold_in(own, 2), (rows, 1), 0, top)
    return jnp.take_along_axis(grid, (jnp.arange(top)[None, :] + offset_by) % top, axis=1)


def load_shares(count, total, limit, slope, full):
    loads = [(1 << 20) // math.isqrt(standing ** slope) + 1 for standing in range(1, count + 1)]
    largest = limit if full else min(limit, max(-(-total // count), total * loads[0] // sum(loads)))
    least = 1 if total - largest >= count - 1 else 0
    counts, rest = [largest] + [least] * (count - 1), total - largest - least * (count - 1)
    while rest > 0:
        free = [i for i in range(1, count) if counts[i] < largest] or [i for i in range(1, count) if counts[i] < limit]
        mass, remaining = sum([loads[i] for i in free]), rest
        for i in free:
            extra = min(limit - counts[i], max(1, remaining * loads[i] // mass), rest)
            counts[i] = counts[i] + extra
            rest = rest - extra
    return np.array(counts)


def scatter_about(own_key, extent, scale, reach, shards=(), held_as=jnp.bfloat16):
    factor_of = shard_levels(own_key, extent, shards, -0.22, 0.18) if shards else 1.0
    entries = jax.random.normal(own_key, extent, jnp.float32) * scale * factor_of
    return jnp.minimum(jnp.maximum(entries, -reach), reach).astype(held_as)


def setup_inputs(seed: int = 0) -> dict:
    streams_of = jax.random.split(jax.random.key(seed), 11)
    tokens = scatter_about(streams_of[0], (TOKENS, D), 0.5, 3.0, ((0, 32),))
    act_scale = draw_act_scale(jax.random.fold_in(streams_of[10], 71), 0)
    routes_keys = jax.random.split(jax.random.fold_in(streams_of[2], 1), TOKENS // TOK_DEV)
    routes_turns = jax.random.permutation(jax.random.fold_in(streams_of[2], 3), TOKENS // TOK_DEV)
    routes = jax.vmap(lambda own, number: assign_block(jax.random.fold_in(streams_of[2], 2), own, number, TOK_DEV, EXPERTS, TOP, CAP, 1))(routes_keys, routes_turns).reshape((TOKENS, TOP))
    combine = jnp.clip(0.1 + 0.5 * jax.random.uniform(streams_of[3], (TOKENS, TOP), jnp.float32) ** shard_levels(streams_of[3], (TOKENS, TOP), ((0, 32),), -0.2, 0.2), 0.1, 0.6)
    w_gate = scatter_about(streams_of[4], (EXPERTS, D, FF), (4 * D) ** -0.5, 0.046875, ((0, 32),))
    gate_scale = draw_gate_scale(jax.random.fold_in(streams_of[10], 71), 0)
    w_up = scatter_about(streams_of[6], (EXPERTS, D, FF), (4 * D) ** -0.5, 0.046875, ((0, 32),))
    up_scale = draw_up_scale(jax.random.fold_in(streams_of[10], 71), 0)
    w_down = scatter_about(streams_of[8], (EXPERTS, FF, D), (4 * FF) ** -0.5, 0.09375, ((0, 32),))
    down_scale = draw_down_scale(jax.random.fold_in(streams_of[10], 71), 0)
    return dict(tokens=tokens, act_scale=act_scale, routes=routes, combine=combine, w_gate=w_gate, gate_scale=gate_scale, w_up=w_up, up_scale=up_scale, w_down=w_down, down_scale=down_scale)


def expand_scale(scale_table):
    return jnp.repeat(jnp.repeat(scale_table, BLOCK, axis=0), BLOCK, axis=1)


def dequantize(weight, scale_table):
    return (weight.astype(jnp.float32) * expand_scale(scale_table)).astype(jnp.bfloat16)


def reference(tokens, act_scale, routes, combine, w_gate, gate_scale, w_up, up_scale, w_down, down_scale):
    inputs = (tokens.astype(jnp.float32) * jnp.repeat(act_scale, BLOCK, axis=1)).astype(jnp.bfloat16)
    flat_routes = routes.reshape(-1).astype(jnp.int32)
    flat_weight = combine.reshape(-1)
    owner_row = (jnp.arange(TOKENS * TOP) // TOP).astype(jnp.int32)
    slot_total = EXPERTS * CAP

    def visit_expert(expert_id, running):
        hits = flat_routes == expert_id
        hit_count = jnp.sum(hits.astype(jnp.int32))
        picked_pairs = jnp.nonzero(hits, size=slot_total, fill_value=0)[0].astype(jnp.int32)
        present = jnp.arange(slot_total).astype(jnp.int32) < hit_count
        target_rows = owner_row[picked_pairs]
        row_block = inputs[target_rows]
        gate_full = dequantize(lax.dynamic_index_in_dim(w_gate, expert_id, 0, keepdims=False),
                               lax.dynamic_index_in_dim(gate_scale, expert_id, 0, keepdims=False))
        up_full = dequantize(lax.dynamic_index_in_dim(w_up, expert_id, 0, keepdims=False),
                             lax.dynamic_index_in_dim(up_scale, expert_id, 0, keepdims=False))
        down_full = dequantize(lax.dynamic_index_in_dim(w_down, expert_id, 0, keepdims=False),
                               lax.dynamic_index_in_dim(down_scale, expert_id, 0, keepdims=False))
        gate_value = jnp.dot(row_block, gate_full, preferred_element_type=jnp.float32)
        up_value = jnp.dot(row_block, up_full, preferred_element_type=jnp.float32)
        hidden = (jax.nn.silu(gate_value) * up_value).astype(jnp.bfloat16)
        expert_out = jnp.dot(hidden, down_full, preferred_element_type=jnp.float32).astype(jnp.bfloat16)
        pair_weight = jnp.where(present, flat_weight[picked_pairs], jnp.zeros_like(flat_weight[picked_pairs]))
        return running.at[target_rows].add(pair_weight[:, None] * expert_out.astype(jnp.float32))

    start = jnp.zeros((TOKENS, D), jnp.float32)
    running = lax.fori_loop(0, EXPERTS, visit_expert, start)
    return running.astype(jnp.bfloat16)
```

```python
import jax
import jax.numpy as jnp
from jax import lax
from jax.sharding import PartitionSpec as P

AXES = ("node", "local")


def dequantize(weight, scale_table, scale_block):
    row_count, col_count = weight.shape
    scale_bf = scale_table.astype(jnp.bfloat16)
    shaped = weight.reshape(
        row_count // scale_block, scale_block, col_count // scale_block, scale_block
    )
    return (shaped * scale_bf[:, None, :, None]).reshape(row_count, col_count)


def local(
    tokens, act_scale, routes, combine, w_gate, gate_scale, w_up, up_scale, w_down, down_scale
):
    tok_rows, width = tokens.shape
    top = routes.shape[1]
    block = width // act_scale.shape[1]
    experts = lax.axis_size("node") * lax.axis_size("local")
    capacity = 5 * tok_rows * top // (4 * experts)
    me = lax.axis_index("node") * lax.axis_size("local") + lax.axis_index("local")
    large = experts * tok_rows * width > 1 << 25
    chunks = 7 if large else 4
    step = width // chunks
    inputs = (
        tokens.reshape(tok_rows, -1, block) * act_scale.astype(jnp.bfloat16)[:, :, None]
    ).reshape(tok_rows, width)
    small = jnp.concatenate([routes.astype(jnp.float32), combine], axis=1)
    small = lax.all_gather(small, AXES, axis=0, tiled=False)
    match = small[:, :, :top] == me.astype(jnp.float32)
    hit = jnp.any(match, axis=2)
    weight = jnp.sum(jnp.where(match, small[:, :, top:], 0.0), axis=2)
    earlier = jnp.triu(jnp.ones((tok_rows, tok_rows), jnp.bfloat16), 1)
    rank = jnp.dot(
        hit.astype(jnp.bfloat16), earlier, preferred_element_type=jnp.float32
    ).astype(jnp.int32)
    slots = jnp.arange(capacity, dtype=jnp.int32)[None, :, None]
    chosen = hit[:, None, :] & (rank[:, None, :] == slots)
    select = chosen.astype(jnp.bfloat16)
    slot_weight = jnp.sum(jnp.where(chosen, weight[:, None, :], 0.0), axis=2)

    gate_full = dequantize(w_gate[0], gate_scale[0], block)
    up_full = dequantize(w_up[0], up_scale[0], block)
    down_full = dequantize(w_down[0], down_scale[0], block)
    gate_value = 0.0
    up_value = 0.0
    history = []
    for c in range(chunks):
        cols = slice(c * step, (c + 1) * step)
        mine = inputs[:, cols]
        if large and c >= 2:
            mine, history[c - 2] = lax.optimization_barrier((mine, history[c - 2]))
        rows = lax.all_gather(mine, AXES, axis=0, tiled=False)
        picked = jnp.einsum(
            "est,etd->esd", select, rows, preferred_element_type=jnp.float32
        ).astype(jnp.bfloat16).reshape(experts * capacity, step)
        history.append(picked)
        gate_value += jnp.dot(picked, gate_full[cols], preferred_element_type=jnp.float32)
        up_value += jnp.dot(picked, up_full[cols], preferred_element_type=jnp.float32)
    hidden = (jax.nn.silu(gate_value) * up_value).astype(jnp.bfloat16)
    outs = []
    for c in range(chunks):
        cols = slice(c * step, (c + 1) * step)
        rows = jnp.dot(hidden, down_full[:, cols], preferred_element_type=jnp.float32)
        rows = rows.astype(jnp.bfloat16).astype(jnp.float32).reshape(experts, capacity, step)
        rows = (rows * slot_weight[:, :, None]).astype(jnp.bfloat16)
        part = jnp.einsum(
            "est,esd->etd", select, rows, preferred_element_type=jnp.float32
        ).astype(jnp.bfloat16).reshape(experts * tok_rows, step)
        outs.append(lax.psum_scatter(part, AXES, scatter_dimension=0, tiled=True))
    return jnp.concatenate(outs, axis=1)


def solution(mesh):
    rows = P(AXES, None)
    stack = P(AXES, None, None)
    return jax.shard_map(
        local, mesh=mesh, in_specs=(rows,) * 4 + (stack,) * 6, out_specs=rows, check_vma=False
    )
```

```python
import jax
import jax.numpy as jnp
from jax import lax
from jax.sharding import PartitionSpec as P

AXES = ("node", "local")


def dequantize(weight, scale_table, scale_block):
    row_count, col_count = weight.shape
    scale_bf = scale_table.astype(jnp.bfloat16)
    shaped = weight.reshape(
        row_count // scale_block, scale_block, col_count // scale_block, scale_block
    )
    return (shaped * scale_bf[:, None, :, None]).reshape(row_count, col_count)


def local(
    tokens, act_scale, routes, combine, w_gate, gate_scale, w_up, up_scale, w_down, down_scale
):
    tok_rows, width = tokens.shape
    top = routes.shape[1]
    block = width // act_scale.shape[1]
    experts = lax.axis_size("node") * lax.axis_size("local")
    capacity = 5 * tok_rows * top // (4 * experts)
    chunks = 2
    step = width // chunks
    inputs = (
        tokens.reshape(tok_rows, -1, block) * act_scale.astype(jnp.bfloat16)[:, :, None]
    ).reshape(tok_rows, width)

    match = routes.T[None] == jnp.arange(experts, dtype=jnp.int32)[:, None, None]
    hit = jnp.any(match, axis=1)
    weight = jnp.sum(jnp.where(match, combine.T[None], 0.0), axis=1)
    earlier = jnp.triu(jnp.ones((tok_rows, tok_rows), jnp.bfloat16), 1)
    rank = jnp.dot(
        hit.astype(jnp.bfloat16), earlier, preferred_element_type=jnp.float32
    ).astype(jnp.int32)
    slots = jnp.arange(capacity, dtype=jnp.int32)[None, :, None]
    chosen = hit[:, None, :] & (rank[:, None, :] == slots)
    select = chosen.astype(jnp.bfloat16).reshape(experts * capacity, tok_rows)
    coarse = lax.reduce_precision(weight, 8, 7)
    fine = weight - coarse

    def spread(values):
        placed = jnp.where(chosen, values[:, None, :], 0.0)
        return placed.astype(jnp.bfloat16).reshape(experts * capacity, tok_rows)

    coarse, fine = spread(coarse), spread(fine)

    def exchange(rows):
        return lax.all_to_all(
            rows.reshape(experts, capacity, step), AXES, split_axis=0, concat_axis=0, tiled=True
        ).reshape(experts * capacity, step)

    def gather_back(weights, rows):
        return lax.dot_general(
            weights, rows, (((0,), (0,)), ((), ())), preferred_element_type=jnp.float32
        )

    spans = [slice(c * step, (c + 1) * step) for c in range(chunks)]
    arrived = [
        exchange(
            jnp.dot(
                select, inputs[:, cols], preferred_element_type=jnp.float32
            ).astype(jnp.bfloat16)
        )
        for cols in spans
    ]
    gate_full = dequantize(w_gate[0], gate_scale[0], block)
    up_full = dequantize(w_up[0], up_scale[0], block)
    down_full = dequantize(w_down[0], down_scale[0], block)
    gate_value = 0.0
    up_value = 0.0
    for cols, rows in zip(spans, arrived):
        gate_value += jnp.dot(rows, gate_full[cols], preferred_element_type=jnp.float32)
        up_value += jnp.dot(rows, up_full[cols], preferred_element_type=jnp.float32)
    hidden = (jax.nn.silu(gate_value) * up_value).astype(jnp.bfloat16)
    returned = [
        exchange(
            jnp.dot(hidden, down_full[:, cols], preferred_element_type=jnp.float32).astype(
                jnp.bfloat16
            )
        )
        for cols in spans
    ]
    outs = [
        (gather_back(coarse, rows) + gather_back(fine, rows)).astype(jnp.bfloat16)
        for rows in returned
    ]
    return jnp.concatenate(outs, axis=1)


def solution(mesh):
    rows = P(AXES, None)
    stack = P(AXES, None, None)
    return jax.shard_map(
        local, mesh=mesh, in_specs=(rows,) * 4 + (stack,) * 6, out_specs=rows, check_vma=False
    )
```

```python
import jax
import jax.numpy as jnp
from jax import lax
from jax.sharding import PartitionSpec as P

AXES = ("node", "local")


def dequantize(weight, scale_table, scale_block):
    row_count, col_count = weight.shape
    scale_bf = scale_table.astype(jnp.bfloat16)
    shaped = weight.reshape(
        row_count // scale_block, scale_block, col_count // scale_block, scale_block
    )
    return (shaped * scale_bf[:, None, :, None]).reshape(row_count, col_count)


def local(
    tokens, act_scale, routes, combine, w_gate, gate_scale, w_up, up_scale, w_down, down_scale
):
    tok_rows, width = tokens.shape
    top = routes.shape[1]
    block = width // act_scale.shape[1]
    experts = lax.axis_size("node") * lax.axis_size("local")
    capacity = 5 * tok_rows * top // (4 * experts)
    minor = act_scale.shape[1] * 2 // 7 * block
    major = width - act_scale.shape[1] * 3 // 7 * block
    inputs = (
        tokens.reshape(tok_rows, -1, block) * act_scale.astype(jnp.bfloat16)[:, :, None]
    ).reshape(tok_rows, width)

    match = routes.T[None] == jnp.arange(experts, dtype=jnp.int32)[:, None, None]
    hit = jnp.any(match, axis=1)
    weight = jnp.sum(jnp.where(match, combine.T[None], 0.0), axis=1)
    earlier = jnp.triu(jnp.ones((tok_rows, tok_rows), jnp.bfloat16), 1)
    rank = jnp.dot(
        hit.astype(jnp.bfloat16), earlier, preferred_element_type=jnp.float32
    ).astype(jnp.int32)
    slots = jnp.arange(capacity, dtype=jnp.int32)[None, :, None]
    chosen = hit[:, None, :] & (rank[:, None, :] == slots)
    select = chosen.astype(jnp.bfloat16).reshape(experts * capacity, tok_rows)
    coarse = lax.reduce_precision(weight, 8, 7)
    fine = weight - coarse

    def spread(values):
        placed = jnp.where(chosen, values[:, None, :], 0.0)
        return placed.astype(jnp.bfloat16).reshape(experts * capacity, tok_rows)

    shares = jnp.concatenate([spread(coarse), spread(fine)], axis=1)

    def exchange(rows):
        return lax.all_to_all(
            rows.reshape(experts, capacity, -1), AXES, split_axis=0, concat_axis=0, tiled=True
        ).reshape(experts * capacity, -1)

    def gather_back(rows):
        both = lax.dot_general(
            shares, rows, (((0,), (0,)), ((), ())), preferred_element_type=jnp.float32
        )
        return (both[:tok_rows] + both[tok_rows:]).astype(jnp.bfloat16)

    spans = (slice(0, major), slice(major, width))
    placed = [
        jnp.dot(select, inputs[:, cols], preferred_element_type=jnp.float32).astype(jnp.bfloat16)
        for cols in spans
    ]
    gate_full = dequantize(w_gate[0], gate_scale[0], block)
    up_full = dequantize(w_up[0], up_scale[0], block)
    down_full = dequantize(w_down[0], down_scale[0], block)
    arrived = [exchange(rows) for rows in placed]
    gate_value = 0.0
    up_value = 0.0
    for cols, rows in zip(spans, arrived):
        gate_value += jnp.dot(rows, gate_full[cols], preferred_element_type=jnp.float32)
        up_value += jnp.dot(rows, up_full[cols], preferred_element_type=jnp.float32)
    hidden = (jax.nn.silu(gate_value) * up_value).astype(jnp.bfloat16)
    returned = [
        exchange(
            jnp.dot(hidden, down_full[:, cols], preferred_element_type=jnp.float32).astype(
                jnp.bfloat16
            )
        )
        for cols in (slice(0, minor), slice(minor, width))
    ]
    return jnp.concatenate([gather_back(rows) for rows in returned], axis=1)


def solution(mesh):
    rows = P(AXES, None)
    stack = P(AXES, None, None)
    return jax.shard_map(
        local, mesh=mesh, in_specs=(rows,) * 4 + (stack,) * 6, out_specs=rows, check_vma=False
    )
```

```python
import jax
import jax.numpy as jnp
from jax import lax
from jax.sharding import PartitionSpec as P

AXES = ("node", "local")


def dequantize(weight, scale_table, scale_block):
    row_count, col_count = weight.shape
    scale_bf = scale_table.astype(jnp.bfloat16)
    shaped = weight.reshape(
        row_count // scale_block, scale_block, col_count // scale_block, scale_block
    )
    return (shaped * scale_bf[:, None, :, None]).reshape(row_count, col_count)


def local(
    tokens, act_scale, routes, combine, w_gate, gate_scale, w_up, up_scale, w_down, down_scale
):
    tok_rows, width = tokens.shape
    top = routes.shape[1]
    block = width // act_scale.shape[1]
    experts = lax.axis_size("node") * lax.axis_size("local")
    capacity = 5 * tok_rows * top // (4 * experts)
    minor = act_scale.shape[1] * 2 // 7 * block
    major = width - act_scale.shape[1] * 5 // 14 * block
    inputs = (
        tokens.reshape(tok_rows, -1, block) * act_scale.astype(jnp.bfloat16)[:, :, None]
    ).reshape(tok_rows, width)

    match = routes.T[None] == jnp.arange(experts, dtype=jnp.int32)[:, None, None]
    hit = jnp.any(match, axis=1)
    weight = jnp.sum(jnp.where(match, combine.T[None], 0.0), axis=1)
    earlier = jnp.triu(jnp.ones((tok_rows, tok_rows), jnp.bfloat16), 1)
    rank = jnp.dot(
        hit.astype(jnp.bfloat16), earlier, preferred_element_type=jnp.float32
    ).astype(jnp.int32)
    slots = jnp.arange(capacity, dtype=jnp.int32)[None, :, None]
    chosen = hit[:, None, :] & (rank[:, None, :] == slots)
    select = chosen.astype(jnp.bfloat16).reshape(experts * capacity, tok_rows)
    coarse = lax.reduce_precision(weight, 8, 7)
    fine = weight - coarse

    def spread(values):
        placed = jnp.where(chosen, values[:, None, :], 0.0)
        return placed.astype(jnp.bfloat16).reshape(experts * capacity, tok_rows)

    shares = jnp.concatenate([spread(coarse), spread(fine)], axis=1)

    def exchange(rows):
        return lax.all_to_all(
            rows.reshape(experts, capacity, -1), AXES, split_axis=0, concat_axis=0, tiled=True
        ).reshape(experts * capacity, -1)

    def gather_back(rows):
        both = lax.dot_general(
            shares, rows, (((0,), (0,)), ((), ())), preferred_element_type=jnp.float32
        )
        return (both[:tok_rows] + both[tok_rows:]).astype(jnp.bfloat16)

    spans = (slice(0, major), slice(major, width))
    placed = [
        jnp.dot(select, inputs[:, cols], preferred_element_type=jnp.float32).astype(jnp.bfloat16)
        for cols in spans
    ]
    gate_full = dequantize(w_gate[0], gate_scale[0], block)
    up_full = dequantize(w_up[0], up_scale[0], block)
    down_full = dequantize(w_down[0], down_scale[0], block)
    arrived = [exchange(rows) for rows in placed]
    first, second = spans

    def project(rows, cols, full):
        return jnp.dot(rows, full[cols], preferred_element_type=jnp.float32)

    gate_value = project(arrived[0], first, gate_full)
    up_value = project(arrived[0], first, up_full)
    gate_value, up_value, rest = lax.optimization_barrier((gate_value, up_value, arrived[1]))
    gate_value += project(rest, second, gate_full)
    up_value += project(rest, second, up_full)
    hidden = (jax.nn.silu(gate_value) * up_value).astype(jnp.bfloat16)
    returned = [
        exchange(
            jnp.dot(hidden, down_full[:, cols], preferred_element_type=jnp.float32).astype(
                jnp.bfloat16
            )
        )
        for cols in (slice(0, minor), slice(minor, width))
    ]
    return jnp.concatenate([gather_back(rows) for rows in returned], axis=1)


def solution(mesh):
    rows = P(AXES, None)
    stack = P(AXES, None, None)
    return jax.shard_map(
        local, mesh=mesh, in_specs=(rows,) * 4 + (stack,) * 6, out_specs=rows, check_vma=False
    )
```
